512 devices in a mesh: row: 16 (over y, z_lo), col: 32 (over z_hi, x, core).
Axes of the slice: x: 4, y: 4, z: 16 (z_hi: 4, z_lo: 4; z = z_hi * 4 + z_lo), core: 2. Of those that a mesh axis runs over, the one named last changes fastest.
Arguments:
- eigenbasis: float32 [18432, 18432], P('row', 'col'), may hold values from -0.078125 to 0.078125
- eigenvalues: float32 [18432], P('col'), may hold values from 0.02 to 2
- queries: float32 [18432, 256], P('row'), may hold values from -6 to 6
- activations: bfloat16 [16384, 18432], P('row', 'col'), may hold values from -0.078125 to 0.078125
Outputs:
- scores: float32 [16384, 256], P(('row', 'col'))
The draws below stay inside these ranges and needn't reach their ends.
All inputs are finite; a program needn't handle non-finite values.
Results may differ from the reference program's by a relative error of at most 0.0029.
Values may be sent and summed in bfloat16 or wider, within the bound.
A program may use at most 64 MiB of HBM per device.

```python
import math
import jax
import jax.numpy as jnp
from jax import lax

F = 18432
NQ = 256
TOKENS = 16384


def raised(entries, stream_key, source, target, blocks, factor):
    def block_of(axis_at):
        return (jnp.arange(entries.shape[axis_at]) // (entries.shape[axis_at] // blocks)).reshape((-1,) + (1,) * (entries.ndim - 1 - axis_at))

    near = jax.random.permutation(stream_key, blocks)[block_of(target)]
    other_side = (block_of(target) + blocks // 2) % blocks
    return jnp.where((block_of(source) == near) | (block_of(source) == other_side), factor * entries, entries)


def level_of(own_key, shape, shards, smallest, largest):
    gain, own = 1.0, jax.random.fold_in(own_key, 6)
    for axis_at, shards_of in shards:
        heights = jnp.exp(jax.random.uniform(jax.random.fold_in(own, axis_at), (shards_of,), jnp.float32, smallest / len(shards), largest / len(shards)))
        gain = gain * jnp.repeat(heights, shape[axis_at] // shards_of).reshape([-1 if axis == axis_at else 1 for axis in range(len(shape))])
    return gain


def normal_values(key, dims, deviation, bound, pieces=(), dtype=jnp.bfloat16):
    array = jax.random.normal(key, dims, jnp.float32) * deviation
    if len(pieces) > 0:
        array = level_of(key, dims, pieces, -0.22, 0.18) * array
    return jnp.clip(array, min=-bound, max=bound).astype(dtype)


def gaussian_with(stream_key, dims, deviation, most, pieces, heavy, held_as=jnp.bfloat16):
    drawn = deviation * jax.random.normal(stream_key, dims, jnp.float32)
    if pieces:
        drawn = drawn * level_of(stream_key, dims, pieces, -0.22, 0.18)
    return jnp.clip(raised(drawn, jax.random.fold_in(stream_key, 3), *heavy), -most, most).astype(held_as)


def setup_inputs(seed: int = 0) -> dict:
    splits = jax.random.split(jax.random.key(seed), 5)
    eigenbasis = gaussian_with(splits[0], (F, F), F ** -0.5, 0.078125, ((0, 16), (1, 32)), (0, 1, 32, 2.75), jnp.float32)
    eigenvalues = jnp.clip(jnp.exp(math.log(2.0) - 4.6051702 * jax.random.uniform(splits[1], (F,), jnp.float32) ** level_of(splits[1], (F,), ((0, 32),), -0.2, 0.2)), 0.02, 2.0)
    queries = normal_values(splits[2], (F, NQ), 1.0, 6.0, ((0, 16),), jnp.float32)
    activations = gaussian_with(splits[3], (TOKENS, F), (F ** -0.5), 0.078125, ((0, 16), (1, 32)), (1, 0, 32, 2.75))
    return {"eigenbasis": eigenbasis, "eigenvalues": eigenvalues, "queries": queries, "activations": activations}


damping = 0.1


def reference(eigenbasis, eigenvalues, queries, activations):
    rotated = lax.dot_general(eigenbasis, queries, (((0,), (0,)), ((), ())), precision=lax.Precision.HIGHEST, preferred_element_type=jnp.float32)
    scaled = rotated / (eigenvalues[:, None] + damping)
    preconditioned = jnp.dot(eigenbasis, scaled, precision=lax.Precision.HIGHEST, preferred_element_type=jnp.float32).astype(jnp.bfloat16)
    return jnp.dot(activations, preconditioned, preferred_element_type=jnp.float32)
```

```python
import functools

import jax
import jax.numpy as jnp
from jax import lax
from jax.experimental import pallas as pl
from jax.experimental.pallas import tpu as pltpu
from jax.sharding import PartitionSpec as P

damping = 0.1
MESH = pl.DeviceIdType.MESH
f32, bf16 = jnp.float32, jnp.bfloat16
CHUNKS = 2
QC = 128
COLS = 576
WIN = 640


def halves(v):
    hi = v.astype(bf16)
    return hi, (v - hi.astype(f32)).astype(bf16)


def dot(a, b):
    return jnp.dot(a, b, preferred_element_type=f32)


def kernel(
    et_hbm, ev_ref, q_hbm, at_hbm, out_ref,
    et_v, q_v, at_v, eh, el, rot, act,
    ry_tx, ry_rx, rz_tx, rz_rx, st,
    pk_tx, pk_rx, px_tx, px_rx, pz_tx, pz_rx, pm, pc_rx, pc,
    sk_tx, sk_own, sk_rx, sx_tx, sx_own, sx_rx, sz_tx, sz_own, sz_rx,
    load_sem, quad_tx, quad_rx, pair_tx, pair_rx, all_tx, all_rx,
):
    row, col = lax.axis_index("row"), lax.axis_index("col")
    y, zl = row // 4, row % 4
    zh, x, k = col // 8, (col // 2) % 4, col % 2

    def device(y=y, zl=zl, zh=zh, x=x, k=k):
        return (y * 4 + zl, zh * 8 + x * 2 + k)

    turned = device(y=zh, zl=x, zh=y, x=zl)
    stays = (x == zl) & (zh == y)

    loads = [
        pltpu.make_async_copy(q_hbm, q_v, load_sem.at[0]),
        pltpu.make_async_copy(et_hbm, et_v, load_sem.at[1]),
        pltpu.make_async_copy(at_hbm, at_v.at[pl.ds(pl.multiple_of(k * 64, 64), COLS)], load_sem.at[2]),
    ]
    for load in loads:
        load.start()

    barrier = pltpu.get_barrier_semaphore()

    def greet(who):
        pl.semaphore_signal(barrier, inc=1, device_id=who, device_id_type=MESH)

    row_peers = []
    for dy in range(4):
        for dz in range(4):
            if dy or dz:
                row_peers.append(((y + dy) % 4, (zl + dz) % 4))
    for py, pz in row_peers:
        greet(device(y=py, zl=pz))
    greet(device(k=1 - k))
    for d in range(1, 4):
        greet(device(x=(x + d) % 4))
        greet(device(zh=(zh + d) % 4))

    @pl.when(jnp.logical_not(stays))
    def _():
        greet(turned)

    at_v[pl.ds(pl.multiple_of((1 - k) * COLS, 64), 64), :] = jnp.zeros((64, 1024), bf16)

    loads[0].wait()
    qh, ql = halves(q_v[...])
    loads[1].wait()
    tile = 288
    for i in range(COLS // tile):
        rows = pl.ds(i * tile, tile)
        h, l = halves(et_v[rows, :])
        eh[rows, :] = h
        el[rows, :] = l
        rot[rows, :] = dot(h, qh) + dot(h, ql) + dot(l, qh)

    pl.semaphore_wait(barrier, 22 + jnp.where(stays, 0, 1))

    sent = []

    def send(src, dst, tx, rx, who):
        copy = pltpu.make_async_remote_copy(
            src_ref=src, dst_ref=dst, send_sem=tx, recv_sem=rx, device_id=who, device_id_type=MESH
        )
        copy.start()
        sent.append(copy)
        return copy

    def quad(stage, ch, source, target, axis, at):
        copies = []
        for d in range(1, 4):
            to = (at + d) % 4
            copies.append(
                send(source(to), target(d - 1), quad_tx.at[stage, ch, d - 1], quad_rx.at[stage, ch, d - 1],
                     device(**{axis: to}))
            )
        return copies

    def chunk(ch):
        lanes = slice(ch * QC, (ch + 1) * QC)
        ry_tx[ch] = rot[:, lanes].T.reshape(4, 32, COLS)
        copies = quad(0, ch, lambda to: ry_tx.at[ch, to], lambda s: ry_rx.at[ch, s], "y", y)
        yield
        for copy in copies:
            copy.wait_recv()
        total = ry_tx[ch, y] + ry_rx[ch, 0] + ry_rx[ch, 1] + ry_rx[ch, 2]
        rz_tx[ch] = total.reshape(4, 8, COLS)
        copies = quad(1, ch, lambda to: rz_tx.at[ch, to], lambda s: rz_rx.at[ch, s], "zl", zl)
        yield
        for copy in copies:
            copy.wait_recv()
        total = rz_tx[ch, zl] + rz_rx[ch, 0] + rz_rx[ch, 1] + rz_rx[ch, 2]
        st[ch, y, zl] = total / (ev_ref[...] + damping)
        copies = quad(2, ch, lambda to: st.at[ch, y, zl], lambda s: st.at[ch, y, zl], "zl", zl)
        yield
        for copy in copies:
            copy.wait_recv()
        copies = quad(3, ch, lambda to: st.at[ch, y], lambda s: st.at[ch, y], "y", y)
        yield
        for copy in copies:
            copy.wait_recv()
        sh, sl = halves(st[ch].reshape(QC, COLS))
        both = jnp.concatenate([sh, sl], axis=0)

        def window(at):
            cols = pl.ds(pl.multiple_of(at * 512, 128), WIN)
            wide = dot(both, eh[:, cols])
            return wide[:QC] + wide[QC:] + dot(sh, el[:, cols])

        pk_tx[ch] = window(1 - k)
        copy = send(pk_tx.at[ch], pk_rx.at[ch], pair_tx.at[0, ch], pair_rx.at[0, ch], device(k=1 - k))
        own = window(k)
        copy.wait_recv()
        px_tx[ch] = (own + pk_rx[ch]).reshape(4, 32, WIN)
        copies = quad(4, ch, lambda to: px_tx.at[ch, to], lambda s: px_rx.at[ch, s], "x", x)
        yield
        for copy in copies:
            copy.wait_recv()
        total = px_tx[ch, x] + px_rx[ch, 0] + px_rx[ch, 1] + px_rx[ch, 2]
        pz_tx[ch] = total.reshape(4, 8, WIN)
        copies = quad(5, ch, lambda to: pz_tx.at[ch, to], lambda s: pz_rx.at[ch, s], "zh", zh)
        yield
        for copy in copies:
            copy.wait_recv()
        total = pz_tx[ch, zh] + pz_rx[ch, 0] + pz_rx[ch, 1] + pz_rx[ch, 2]
        pm[ch] = jnp.concatenate([total[:, :384], total[:, 256:]], axis=0).astype(bf16)
        moved = pltpu.make_async_remote_copy(
            src_ref=pm.at[ch], dst_ref=pc_rx.at[ch, x, zh], send_sem=pair_tx.at[1, ch], recv_sem=pair_rx.at[1, ch],
            device_id=turned, device_id_type=MESH,
        )

        @pl.when(jnp.logical_not(stays))
        def _():
            moved.start()

        @pl.when(stays)
        def _():
            pc_rx[ch, x, zh] = pm[ch]

        yield

        @pl.when(jnp.logical_not(stays))
        def _():
            moved.wait()

        copies = []
        for n, (py, pz) in enumerate(row_peers):
            here = pc_rx.at[ch, zl, y]
            copies.append(send(here, here, all_tx.at[ch, n], all_rx.at[ch, n], device(y=py, zl=pz)))
        yield
        for copy in copies:
            copy.wait_recv()
        for a in range(4):
            for b in range(4):
                v = pc_rx[ch, a, b].astype(f32)
                rows = slice(32 * a + 8 * b, 32 * a + 8 * b + 8)
                pc[ch, rows, 0:384] = v[0:8]
                pc[ch, rows, 384:640] = v[8:16, 128:384]
        precond = pc[ch].astype(bf16)

        def scores(half):
            tokens = act[half].reshape(512, WIN)
            return lax.dot_general(tokens, precond, (((1,), (1,)), ((), ())), preferred_element_type=f32)

        sk_tx[ch] = scores(1 - k)
        copy = send(sk_tx.at[ch], sk_rx.at[ch], pair_tx.at[2, ch], pair_rx.at[2, ch], device(k=1 - k))
        own = scores(k)
        copy.wait_recv()
        total = (own + sk_rx[ch]).reshape(4, 128, QC)
        sx_own[ch] = total
        sx_tx[ch] = total.astype(bf16)
        copies = quad(6, ch, lambda to: sx_tx.at[ch, to], lambda s: sx_rx.at[ch, s], "x", x)
        yield
        for copy in copies:
            copy.wait_recv()
        total = sx_own[ch, x]
        for s in range(3):
            total = total + sx_rx[ch, s].astype(f32)
        total = total.reshape(4, 32, QC)
        sz_own[ch] = total
        sz_tx[ch] = total.astype(bf16)
        copies = quad(7, ch, lambda to: sz_tx.at[ch, to], lambda s: sz_rx.at[ch, s], "zh", zh)
        yield
        for copy in copies:
            copy.wait_recv()
        total = sz_own[ch, zh]
        for s in range(3):
            total = total + sz_rx[ch, s].astype(f32)
        out_ref[:, lanes] = total

    running = [chunk(ch) for ch in range(CHUNKS)]
    turn = 0
    while running:
        for one in list(running):
            try:
                next(one)
            except StopIteration:
                running.remove(one)
        if turn == 0:
            loads[2].wait()
            for t in range(8):
                block = at_v[:, t * 128 : (t + 1) * 128].T
                for i in range(4):
                    c = 4 * t + i
                    act[c % 2, (c // 2) % 4, c // 8] = block[32 * i : 32 * i + 32]
        turn += 1
    for copy in sent:
        copy.wait_send()


def per_device(eigenbasis, eigenvalues, queries, activations):
    n = CHUNKS
    dma = pltpu.SemaphoreType.DMA
    V = pltpu.VMEM
    any_space = pl.BlockSpec(memory_space=pl.ANY)
    vmem = pl.BlockSpec(memory_space=V)
    return pl.pallas_call(
        kernel,
        out_shape=jax.ShapeDtypeStruct((32, 256), f32),
        in_specs=[any_space, vmem, any_space, any_space],
        out_specs=vmem,
        scratch_shapes=[
            V((COLS, 1152), f32), V((1152, 256), f32), V((WIN, 1024), bf16),
            V((COLS, 1152), bf16), V((COLS, 1152), bf16), V((COLS, 256), f32), V((2, 4, 4, 32, WIN), bf16),
            V((n, 4, 32, COLS), f32), V((n, 3, 32, COLS), f32), V((n, 4, 8, COLS), f32), V((n, 3, 8, COLS), f32),
            V((n, 4, 4, 8, COLS), f32),
            V((n, QC, WIN), f32), V((n, QC, WIN), f32), V((n, 4, 32, WIN), f32), V((n, 3, 32, WIN), f32),
            V((n, 4, 8, WIN), f32), V((n, 3, 8, WIN), f32), V((n, 16, 384), bf16), V((n, 4, 4, 16, 384), bf16),
            V((n, QC, WIN), f32),
            V((n, 512, QC), f32), V((1, 8, 128), f32), V((n, 512, QC), f32),
            V((n, 4, 128, QC), bf16), V((n, 4, 128, QC), f32), V((n, 3, 128, QC), bf16),
            V((n, 4, 32, QC), bf16), V((n, 4, 32, QC), f32), V((n, 3, 32, QC), bf16),
            dma((3,)), dma((8, n, 3)), dma((8, n, 3)), dma((3, n)), dma((3, n)), dma((n, 15)), dma((n, 15)),
        ],
        compiler_params=pltpu.CompilerParams(
            collective_id=1, has_side_effects=True, vmem_limit_bytes=56 * 1024 * 1024
        ),
    )(eigenbasis.T, eigenvalues.reshape(1, -1), queries, activations.T)


def solution(mesh):
    placed = (P("row", "col"), P("col"), P("row", None), P("row", "col"))
    return jax.shard_map(
        per_device, mesh=mesh, in_specs=placed, out_specs=P(("row", "col"), None), check_vma=False
    )
```

```python
import functools

import jax
import jax.numpy as jnp
from jax import lax
from jax.experimental import pallas as pl
from jax.experimental.pallas import tpu as pltpu
from jax.sharding import PartitionSpec as P

damping = 0.1
MESH = pl.DeviceIdType.MESH
f32, bf16 = jnp.float32, jnp.bfloat16
CHUNKS = 2
QC = 128
COLS = 576
EIG = ((0, 256), (256, 576))
WIDE = ((0, 256), (256, 640))
PACK = (128, 256)
WIN = 640


def halves(v):
    hi = v.astype(bf16)
    return hi, (v - hi.astype(f32)).astype(bf16)


def dot(a, b):
    return jnp.dot(a, b, preferred_element_type=f32)


def kernel(
    et_hbm, ev_ref, q_hbm, at_hbm, out_ref,
    et_v, q_v, at_v, eh, el, rot, act,
    ry_tx, ry_rx, rz_tx, rz_rx, st,
    pk_tx, pk_rx, px_tx, px_rx, pz_tx, pz_rx, pm, pc_rx, pc,
    sk_tx, sk_rx, sx_tx, sx_own, sx_rx, sz_tx, sz_own, sz_rx,
    load_sem, quad_tx, quad_rx, pair_tx, pair_rx, turn_tx, turn_rx, all_tx, all_rx,
):
    row, col = lax.axis_index("row"), lax.axis_index("col")
    y, zl = row // 4, row % 4
    zh, x, k = col // 8, (col // 2) % 4, col % 2

    def device(y=y, zl=zl, zh=zh, x=x, k=k):
        return (y * 4 + zl, zh * 8 + x * 2 + k)

    turned = device(y=zh, zl=x, zh=y, x=zl)
    stays = (x == zl) & (zh == y)

    loads = [
        pltpu.make_async_copy(q_hbm, q_v, load_sem.at[0]),
        pltpu.make_async_copy(et_hbm, et_v, load_sem.at[1]),
        pltpu.make_async_copy(at_hbm, at_v.at[pl.ds(pl.multiple_of(k * 64, 64), COLS)], load_sem.at[2]),
    ]
    loads[0].start()
    loads[1].start()

    barrier = pltpu.get_barrier_semaphore()

    def greet(who):
        pl.semaphore_signal(barrier, inc=1, device_id=who, device_id_type=MESH)

    row_peers = []
    for dy in range(4):
        for dz in range(4):
            if dy or dz:
                row_peers.append(((y + dy) % 4, (zl + dz) % 4))
    for py, pz in row_peers:
        greet(device(y=py, zl=pz))
    greet(device(k=1 - k))
    for d in range(1, 4):
        greet(device(x=(x + d) % 4))
        greet(device(zh=(zh + d) % 4))

    @pl.when(jnp.logical_not(stays))
    def _():
        greet(turned)

    loads[2].start()
    at_v[pl.ds(pl.multiple_of((1 - k) * COLS, 64), 64), :] = jnp.zeros((64, 1024), bf16)

    loads[0].wait()
    qh, ql = halves(q_v[...])
    loads[1].wait()
    for lo, hi in EIG:
        h, l = halves(et_v[lo:hi, :])
        eh[lo:hi, :] = h
        el[lo:hi, :] = l
        rot[lo:hi, :] = dot(h, qh) + dot(h, ql) + dot(l, qh)

    pl.semaphore_wait(barrier, 22 + jnp.where(stays, 0, 1))

    sent = []

    def send(src, dst, tx, rx, who):
        copy = pltpu.make_async_remote_copy(
            src_ref=src, dst_ref=dst, send_sem=tx, recv_sem=rx, device_id=who, device_id_type=MESH
        )
        copy.start()
        sent.append(copy)
        return copy

    def quad(stage, ch, part, source, target, axis, at):
        copies = []
        for d in range(1, 4):
            to = (at + d) % 4
            copies.append(
                send(source(to), target(d - 1), quad_tx.at[stage, ch, part, d - 1], quad_rx.at[stage, ch, part, d - 1],
                     device(**{axis: to}))
            )
        return copies

    def arrive(copies):
        for copy in copies:
            copy.wait_recv()

    def rotate(ch, p):
        lanes = slice(ch * QC, (ch + 1) * QC)
        lo, hi = EIG[p]
        tx, rx, tz, rz, s = ry_tx[p], ry_rx[p], rz_tx[p], rz_rx[p], st[p]
        tx[ch] = rot[lo:hi, lanes].T.reshape(4, 32, hi - lo)
        copies = quad(0, ch, p, lambda to: tx.at[ch, to], lambda i: rx.at[ch, i], "y", y)
        yield
        arrive(copies)
        total = tx[ch, y] + rx[ch, 0] + rx[ch, 1] + rx[ch, 2]
        tz[ch] = total.reshape(4, 8, hi - lo)
        copies = quad(1, ch, p, lambda to: tz.at[ch, to], lambda i: rz.at[ch, i], "zl", zl)
        yield
        arrive(copies)
        total = tz[ch, zl] + rz[ch, 0] + rz[ch, 1] + rz[ch, 2]
        s[ch, y, zl] = total / (ev_ref[...].reshape(1, COLS)[:, lo:hi] + damping)
        copies = quad(2, ch, p, lambda to: s.at[ch, y, zl], lambda i: s.at[ch, y, zl], "zl", zl)
        yield
        arrive(copies)
        copies = quad(3, ch, p, lambda to: s.at[ch, y], lambda i: s.at[ch, y], "y", y)
        yield
        arrive(copies)

    def expand(ch, state):
        pieces = []
        for p, (lo, hi) in enumerate(EIG):
            sh, sl = halves(st[p][ch].reshape(QC, hi - lo))
            pieces.append((lo, hi, sh, jnp.concatenate([sh, sl], axis=0)))

        def window(at, p):
            first, last = WIDE[p]
            cols = pl.ds(pl.multiple_of(at * 512 + first, 128), last - first)
            total = None
            for lo, hi, sh, both in pieces:
                wide = dot(both, eh[lo:hi, cols])
                term = wide[:QC] + wide[QC:] + dot(sh, el[lo:hi, cols])
                total = term if total is None else total + term
            return total

        for p in range(2):
            pk_tx[p][ch] = window(1 - k, p)
            state[ch, p] = send(
                pk_tx[p].at[ch], pk_rx[p].at[ch], pair_tx.at[p, ch], pair_rx.at[p, ch], device(k=1 - k)
            )
        for p in range(2):
            first, last = WIDE[p]
            px_tx[p][ch] = window(k, p).reshape(4, 32, last - first)

    def collect(ch, p, state):
        first, last = WIDE[p]
        width = last - first
        tx, rx, tz, rz = px_tx[p], px_rx[p], pz_tx[p], pz_rx[p]
        state[ch, p].wait_recv()
        tx[ch] = tx[ch] + pk_rx[p][ch].reshape(4, 32, width)
        copies = quad(4, ch, p, lambda to: tx.at[ch, to], lambda i: rx.at[ch, i], "x", x)
        yield
        arrive(copies)
        total = tx[ch, x] + rx[ch, 0] + rx[ch, 1] + rx[ch, 2]
        tz[ch] = total.reshape(4, 8, width)
        copies = quad(5, ch, p, lambda to: tz.at[ch, to], lambda i: rz.at[ch, i], "zh", zh)
        yield
        arrive(copies)
        total = tz[ch, zh] + rz[ch, 0] + rz[ch, 1] + rz[ch, 2]
        pm[p][ch] = jnp.concatenate([total[:, : PACK[p]], total[:, width - PACK[p] :]], axis=0).astype(bf16)
        moved = pltpu.make_async_remote_copy(
            src_ref=pm[p].at[ch], dst_ref=pc_rx[p].at[ch, x, zh], send_sem=turn_tx.at[p, ch],
            recv_sem=turn_rx.at[p, ch], device_id=turned, device_id_type=MESH,
        )

        @pl.when(jnp.logical_not(stays))
        def _():
            moved.start()

        @pl.when(stays)
        def _():
            pc_rx[p][ch, x, zh] = pm[p][ch]

        yield

        @pl.when(jnp.logical_not(stays))
        def _():
            moved.wait()

        copies = []
        here = pc_rx[p].at[ch, zl, y]
        for n, (py, pz) in enumerate(row_peers):
            copies.append(send(here, here, all_tx.at[ch, p, n], all_rx.at[ch, p, n], device(y=py, zl=pz)))
        yield
        arrive(copies)
        for a in range(4):
            for b in range(4):
                v = pc_rx[p][ch, a, b].astype(f32)
                rows = slice(32 * a + 8 * b, 32 * a + 8 * b + 8)
                pc[ch, rows, first : first + PACK[p]] = v[0:8]
                pc[ch, rows, last - PACK[p] : last] = v[8:16]

    def score(ch, state):
        precond = pc[ch].astype(bf16)

        def scores(half):
            tokens = act[half].reshape(512, WIN)
            return lax.dot_general(tokens, precond, (((1,), (1,)), ((), ())), preferred_element_type=f32)

        sk_tx[ch] = scores(1 - k)
        state[ch] = send(sk_tx.at[ch], sk_rx.at[ch], pair_tx.at[2, ch], pair_rx.at[2, ch], device(k=1 - k))
        sx_own[ch] = scores(k).reshape(4, 128, QC)

    def finish(ch, state):
        lanes = slice(ch * QC, (ch + 1) * QC)
        state[ch].wait_recv()
        total = sx_own[ch] + sk_rx[ch].reshape(4, 128, QC)
        sx_own[ch] = total
        sx_tx[ch] = total.astype(bf16)
        copies = quad(6, ch, 0, lambda to: sx_tx.at[ch, to], lambda s: sx_rx.at[ch, s], "x", x)
        yield
        arrive(copies)
        total = sx_own[ch, x]
        for s in range(3):
            total = total + sx_rx[ch, s].astype(f32)
        total = total.reshape(4, 32, QC)
        sz_own[ch] = total
        sz_tx[ch] = total.astype(bf16)
        copies = quad(7, ch, 0, lambda to: sz_tx.at[ch, to], lambda s: sz_rx.at[ch, s], "zh", zh)
        yield
        arrive(copies)
        total = sz_own[ch, zh]
        for s in range(3):
            total = total + sz_rx[ch, s].astype(f32)
        out_ref[:, lanes] = total

    def step(streams):
        for one in streams:
            next(one, None)

    summed = {}
    first = [[rotate(ch, p) for p in range(2)] for ch in range(CHUNKS)]
    for stage in range(4):
        step(first[0] + first[1])
        if stage == 1:
            loads[2].wait()
            for t in range(8):
                block = at_v[:, t * 128 : (t + 1) * 128].T
                for i in range(4):
                    c = 4 * t + i
                    act[c % 2, (c // 2) % 4, c // 8] = block[32 * i : 32 * i + 32]
    for ch in range(CHUNKS):
        step(first[ch])
        expand(ch, summed)
    second = [[collect(ch, p, summed) for p in range(2)] for ch in range(CHUNKS)]
    for stage in range(4):
        step(second[0] + second[1])
    for ch in range(CHUNKS):
        step(second[ch])
        score(ch, summed)
    third = [finish(ch, summed) for ch in range(CHUNKS)]
    step(third)
    for copy in sent:
        copy.wait_send()
    sent.clear()
    step(third)
    step(third)
    for copy in sent:
        copy.wait_send()


def per_device(eigenbasis, eigenvalues, queries, activations):
    n = CHUNKS
    dma = pltpu.SemaphoreType.DMA
    V = pltpu.VMEM

    def parts(lanes, *lead):
        return [V((n, *lead, hi - lo), f32) for lo, hi in lanes]

    any_space = pl.BlockSpec(memory_space=pl.ANY)
    vmem = pl.BlockSpec(memory_space=V)
    return pl.pallas_call(
        kernel,
        out_shape=jax.ShapeDtypeStruct((32, 256), f32),
        in_specs=[any_space, vmem, any_space, any_space],
        out_specs=vmem,
        scratch_shapes=[
            V((COLS, 1152), f32), V((1152, 256), f32), V((WIN, 1024), bf16),
            V((COLS, 1152), bf16), V((COLS, 1152), bf16), V((COLS, 256), f32), V((2, 4, 4, 32, WIN), bf16),
            parts(EIG, 4, 32), parts(EIG, 3, 32), parts(EIG, 4, 8), parts(EIG, 3, 8), parts(EIG, 4, 4, 8),
            parts(WIDE, QC), parts(WIDE, QC), parts(WIDE, 4, 32), parts(WIDE, 3, 32), parts(WIDE, 4, 8),
            parts(WIDE, 3, 8), [V((n, 16, w), bf16) for w in PACK], [V((n, 4, 4, 16, w), bf16) for w in PACK],
            V((n, QC, WIN), f32),
            V((n, 512, QC), f32), V((n, 512, QC), f32),
            V((n, 4, 128, QC), bf16), V((n, 4, 128, QC), f32), V((n, 3, 128, QC), bf16),
            V((n, 4, 32, QC), bf16), V((n, 4, 32, QC), f32), V((n, 3, 32, QC), bf16),
            dma((3,)), dma((8, n, 2, 3)), dma((8, n, 2, 3)), dma((3, n)), dma((3, n)), dma((2, n)), dma((2, n)),
            dma((n, 2, 15)), dma((n, 2, 15)),
        ],
        compiler_params=pltpu.CompilerParams(
            collective_id=1, has_side_effects=True, vmem_limit_bytes=56 * 1024 * 1024
        ),
    )(eigenbasis.T, eigenvalues, queries, activations.T)


def solution(mesh):
    placed = (P("row", "col"), P("col"), P("row", None), P("row", "col"))
    return jax.shard_map(
        per_device, mesh=mesh, in_specs=placed, out_specs=P(("row", "col"), None), check_vma=False
    )
```

```python
import functools

import jax
import jax.numpy as jnp
from jax import lax
from jax.experimental import pallas as pl
from jax.experimental.pallas import tpu as pltpu
from jax.sharding import PartitionSpec as P

damping = 0.1
MESH = pl.DeviceIdType.MESH
f32, bf16 = jnp.float32, jnp.bfloat16
CHUNKS = 2
QC = 128
COLS = 576
EIG = ((0, 256), (256, 576))
WIDE = ((0, 256), (256, 640))
PACK = (128, 256)
WIN = 640


def halves(v):
    hi = v.astype(bf16)
    return hi, (v - hi.astype(f32)).astype(bf16)


def dot(a, b):
    return jnp.dot(a, b, preferred_element_type=f32)


def kernel(
    et_hbm, ev_ref, q_hbm, at_hbm, out_ref,
    et_v, q_v, at_v, eh, el, rot, act,
    ry_tx, ry_rx, rz_tx, rz_rx, st,
    pk_tx, pk_rx, px_tx, px_rx, pz_tx, pz_rx, pm, pc_rx, pc,
    sk_tx, sk_rx, sx_tx, sx_own, sx_rx, sz_tx, sz_own, sz_rx,
    load_sem, quad_tx, quad_rx, pair_tx, pair_rx, half_tx, half_rx, turn_tx, turn_rx, all_tx, all_rx,
):
    row, col = lax.axis_index("row"), lax.axis_index("col")
    y, zl = row // 4, row % 4
    zh, x, k = col // 8, (col // 2) % 4, col % 2

    def device(y=y, zl=zl, zh=zh, x=x, k=k):
        return (y * 4 + zl, zh * 8 + x * 2 + k)

    to_y = (y + x - zl + 6) % 4
    to_zl = (zh - y + 5 + zl // 2) % 4
    from_x = (x + y - zh + 6) % 4
    from_zh = (zh + zl + 7 - x // 2) % 4

    loads = [
        pltpu.make_async_copy(q_hbm, q_v, load_sem.at[0]),
        *(
            pltpu.make_async_copy(et_hbm.at[pl.ds(lo, hi - lo)], et_v.at[pl.ds(lo, hi - lo)], load_sem.at[1 + p])
            for p, (lo, hi) in enumerate(EIG)
        ),
        pltpu.make_async_copy(at_hbm, at_v.at[pl.ds(pl.multiple_of(k * 64, 64), COLS)], load_sem.at[3]),
    ]
    for load in loads[:3]:
        load.start()

    barrier = pltpu.get_barrier_semaphore()

    def greet(who):
        pl.semaphore_signal(barrier, inc=1, device_id=who, device_id_type=MESH)

    row_peers = [((y + dy) % 4, (zl + dz) % 4) for dz in (2, 1, 3, 0) for dy in (2, 1, 3, 0)][:15]
    greet(device(x=from_x, y=zh, zh=from_zh, zl=x))
    for d in (2, 1, 3):
        greet(device(zh=(zh + d) % 4))
    for py, pz in row_peers:
        greet(device(y=py, zl=pz))
    for d in (2, 1, 3):
        greet(device(x=(x + d) % 4))
    greet(device(k=1 - k))

    loads[3].start()
    at_v[pl.ds(pl.multiple_of((1 - k) * COLS, 64), 64), :] = jnp.zeros((64, 1024), bf16)

    loads[0].wait()
    qh, ql = halves(q_v[...])

    def rotated(p):
        lo, hi = EIG[p]
        loads[1 + p].wait()
        h, l = halves(et_v[lo:hi, :])
        eh[lo:hi, :] = h
        el[lo:hi, :] = l
        rot[lo:hi, :] = dot(h, qh) + dot(h, ql) + dot(l, qh)

    rotated(0)
    pl.semaphore_wait(barrier, 23)

    sent = []

    def send(src, dst, tx, rx, who):
        copy = pltpu.make_async_remote_copy(
            src_ref=src, dst_ref=dst, send_sem=tx, recv_sem=rx, device_id=who, device_id_type=MESH
        )
        copy.start()
        sent.append(copy)
        return copy

    def quad(stage, ch, part, source, target, axis, at):
        copies = []
        for d in range(1, 4):
            to = (at + d) % 4
            copies.append(
                send(source(to), target(d - 1), quad_tx.at[stage, ch, part, d - 1], quad_rx.at[stage, ch, part, d - 1],
                     device(**{axis: to}))
            )
        return copies

    def arrive(copies):
        for copy in copies:
            copy.wait_recv()

    def rotate(ch, p):
        lanes = slice(ch * QC, (ch + 1) * QC)
        lo, hi = EIG[p]
        near, far = (("zl", zl), ("y", y))[:: 1 if p == 0 else -1]
        tx, rx, tz, rz, s = ry_tx[p], ry_rx[p], rz_tx[p], rz_rx[p], st[p]
        i, j = near[1], far[1]
        tx[ch] = rot[lo:hi, lanes].T.reshape(4, 32, hi - lo)
        copies = quad(0, ch, p, lambda to: tx.at[ch, to], lambda n: rx.at[ch, n], *near)
        yield
        arrive(copies)
        total = tx[ch, i] + rx[ch, 0] + rx[ch, 1] + rx[ch, 2]
        tz[ch] = total.reshape(4, 8, hi - lo)
        copies = quad(1, ch, p, lambda to: tz.at[ch, to], lambda n: rz.at[ch, n], *far)
        yield
        arrive(copies)
        total = tz[ch, j] + rz[ch, 0] + rz[ch, 1] + rz[ch, 2]
        s[ch, i, j] = total / (ev_ref[...].reshape(1, COLS)[:, lo:hi] + damping)
        copies = quad(2, ch, p, lambda to: s.at[ch, i, j], lambda n: s.at[ch, i, j], *far)
        yield
        arrive(copies)
        copies = quad(3, ch, p, lambda to: s.at[ch, i], lambda n: s.at[ch, i], *near)
        yield
        arrive(copies)

    def expand(ch, part, state):
        lo, hi = EIG[part]
        sh, sl = halves(st[part][ch].reshape(QC, hi - lo))
        both = jnp.concatenate([sh, sl], axis=0)

        def window(at, p):
            first, last = WIDE[p]
            cols = pl.ds(pl.multiple_of(at * 512 + first, 128), last - first)
            wide = dot(both, eh[lo:hi, cols])
            return wide[:QC] + wide[QC:] + dot(sh, el[lo:hi, cols])

        for p in range(2):
            if part == 0:
                pk_tx[p][ch] = window(1 - k, p)
            else:
                pk_tx[p][ch] = pk_tx[p][ch] + window(1 - k, p)
                state[ch, p] = send(
                    pk_tx[p].at[ch], pk_rx[p].at[ch], pair_tx.at[p, ch], pair_rx.at[p, ch], device(k=1 - k)
                )
        for p in range(2):
            first, last = WIDE[p]
            own = window(k, p).reshape(4, 32, last - first)
            px_tx[p][ch] = own if part == 0 else px_tx[p][ch] + own

    def collect(ch, p, state):
        first, last = WIDE[p]
        width = last - first
        tx, rx, tz, rz = px_tx[p], px_rx[p], pz_tx[p], pz_rx[p]
        state[ch, p].wait_recv()
        tx[ch] = tx[ch] + pk_rx[p][ch].reshape(4, 32, width)
        copies = quad(4, ch, p, lambda to: tx.at[ch, to], lambda i: rx.at[ch, i], "x", x)
        yield
        arrive(copies)
        total = tx[ch, x] + rx[ch, 0] + rx[ch, 1] + rx[ch, 2]
        tz[ch] = total.reshape(4, 8, width)
        copies = quad(5, ch, p, lambda to: tz.at[ch, to], lambda i: rz.at[ch, i], "zh", zh)
        yield
        arrive(copies)
        total = tz[ch, zh] + rz[ch, 0] + rz[ch, 1] + rz[ch, 2]
        pm[p][ch] = jnp.concatenate([total[:, : PACK[p]], total[:, width - PACK[p] :]], axis=0).astype(bf16)
        moved = send(pm[p].at[ch], pc_rx[p].at[ch, x, zh], turn_tx.at[p, ch], turn_rx.at[p, ch],
                     device(x=zl, y=to_y, zh=y, zl=to_zl))
        yield
        moved.wait_recv()
        here = pc_rx[p].at[ch, from_x, from_zh]
        copies = []
        for n, (py, pz) in enumerate(row_peers):
            copies.append(send(here, here, all_tx.at[ch, p, n], all_rx.at[ch, p, n], device(y=py, zl=pz)))
        yield
        arrive(copies)
        for a in range(4):
            for b in range(4):
                v = pc_rx[p][ch, a, b].astype(f32)
                rows = slice(32 * a + 8 * b, 32 * a + 8 * b + 8)
                pc[ch, rows, first : first + PACK[p]] = v[0:8]
                pc[ch, rows, last - PACK[p] : last] = v[8:16]

    def score(ch, p, state):
        first, last = WIDE[p]
        precond = pc[ch, :, first:last].astype(bf16)

        def scores(core, half):
            tokens = act[core, half, :, :, :, first:last].reshape(256, last - first)
            return lax.dot_general(tokens, precond, (((1,), (1,)), ((), ())), preferred_element_type=f32)

        for h in range(2):
            if p == 0:
                sk_tx[ch, h] = scores(1 - k, h)
            else:
                sk_tx[ch, h] = sk_tx[ch, h] + scores(1 - k, h)
                state[ch, h] = send(
                    sk_tx.at[ch, h], sk_rx.at[ch, h], half_tx.at[ch, h], half_rx.at[ch, h], device(k=1 - k)
                )
        for h in range(2):
            own = scores(k, h).reshape(4, 64, QC)
            sx_own[ch, h] = own if p == 0 else sx_own[ch, h] + own

    def finish(ch, h, state):
        lanes = slice(ch * QC, (ch + 1) * QC)
        state[ch, h].wait_recv()
        total = sx_own[ch, h] + sk_rx[ch, h].reshape(4, 64, QC)
        sx_own[ch, h] = total
        sx_tx[ch, h] = total.astype(bf16)
        copies = quad(6, ch, h, lambda to: sx_tx.at[ch, h, to], lambda s: sx_rx.at[ch, h, s], "x", x)
        yield
        arrive(copies)
        total = sx_own[ch, h, x]
        for s in range(3):
            total = total + sx_rx[ch, h, s].astype(f32)
        total = total.reshape(4, 16, QC)
        sz_own[ch, h] = total
        sz_tx[ch, h] = total.astype(bf16)
        copies = quad(7, ch, h, lambda to: sz_tx.at[ch, h, to], lambda s: sz_rx.at[ch, h, s], "zh", zh)
        yield
        arrive(copies)
        total = sz_own[ch, h, zh]
        for s in range(3):
            total = total + sz_rx[ch, h, s].astype(f32)
        out_ref[16 * h : 16 * h + 16, lanes] = total

    def step(streams):
        for one in streams:
            next(one, None)

    summed = {}
    first = [[rotate(ch, p) for p in range(2)] for ch in range(CHUNKS)]
    step([first[0][0]])
    rotated(1)
    step([first[0][1], first[1][0], first[1][1]])
    for stage in range(1, 4):
        step(first[0] + first[1])
        if stage == 1:
            loads[3].wait()
            for t in range(8):
                block = at_v[:, t * 128 : (t + 1) * 128].T
                for i in range(4):
                    c = 4 * t + i
                    for h in range(2):
                        at = 32 * i + 16 * h
                        act[c % 2, h, (c // 2) % 4, c // 8] = block[at : at + 16]
    for ch in range(CHUNKS):
        for p in range(2):
            step([first[ch][p]])
            expand(ch, p, summed)
    second = [[collect(ch, p, summed) for p in range(2)] for ch in range(CHUNKS)]
    for stage in range(4):
        step(second[0] + second[1])
    for ch in range(CHUNKS):
        for p in range(2):
            step([second[ch][p]])
            score(ch, p, summed)
    third = [finish(ch, h, summed) for ch in range(CHUNKS) for h in range(2)]
    step(third)
    for copy in sent:
        copy.wait_send()
    sent.clear()
    step(third)
    step(third)
    for copy in sent:
        copy.wait_send()


def per_device(eigenbasis, eigenvalues, queries, activations):
    n = CHUNKS
    dma = pltpu.SemaphoreType.DMA
    V = pltpu.VMEM

    def parts(lanes, *lead):
        return [V((n, *lead, hi - lo), f32) for lo, hi in lanes]

    any_space = pl.BlockSpec(memory_space=pl.ANY)
    vmem = pl.BlockSpec(memory_space=V)
    return pl.pallas_call(
        kernel,
        out_shape=jax.ShapeDtypeStruct((32, 256), f32),
        in_specs=[any_space, vmem, any_space, any_space],
        out_specs=vmem,
        scratch_shapes=[
            V((COLS, 1152), f32), V((1152, 256), f32), V((WIN, 1024), bf16),
            V((COLS, 1152), bf16), V((COLS, 1152), bf16), V((COLS, 256), f32), V((2, 2, 4, 4, 16, WIN), bf16),
            parts(EIG, 4, 32), parts(EIG, 3, 32), parts(EIG, 4, 8), parts(EIG, 3, 8), parts(EIG, 4, 4, 8),
            parts(WIDE, QC), parts(WIDE, QC), parts(WIDE, 4, 32), parts(WIDE, 3, 32), parts(WIDE, 4, 8),
            parts(WIDE, 3, 8), [V((n, 16, w), bf16) for w in PACK], [V((n, 4, 4, 16, w), bf16) for w in PACK],
            V((n, QC, WIN), f32),
            V((n, 2, 256, QC), f32), V((n, 2, 256, QC), f32),
            V((n, 2, 4, 64, QC), bf16), V((n, 2, 4, 64, QC), f32), V((n, 2, 3, 64, QC), bf16),
            V((n, 2, 4, 16, QC), bf16), V((n, 2, 4, 16, QC), f32), V((n, 2, 3, 16, QC), bf16),
            dma((4,)), dma((8, n, 2, 3)), dma((8, n, 2, 3)), dma((2, n)), dma((2, n)), dma((n, 2)), dma((n, 2)),
            dma((2, n)), dma((2, n)), dma((n, 2, 15)), dma((n, 2, 15)),
        ],
        compiler_params=pltpu.CompilerParams(
            collective_id=1, has_side_effects=True, vmem_limit_bytes=56 * 1024 * 1024
        ),
    )(eigenbasis.T, eigenvalues, queries, activations.T)


def solution(mesh):
    placed = (P("row", "col"), P("col"), P("row", None), P("row", "col"))
    return jax.shard_map(
        per_device, mesh=mesh, in_specs=placed, out_specs=P(("row", "col"), None), check_vma=False
    )
```

```python
import functools

import jax
import jax.numpy as jnp
from jax import lax
from jax.experimental import pallas as pl
from jax.experimental.pallas import tpu as pltpu
from jax.sharding import PartitionSpec as P

damping = 0.1
MESH = pl.DeviceIdType.MESH
f32, bf16 = jnp.float32, jnp.bfloat16
CHUNKS = 2
QC = 128
COLS = 576
EIG = ((0, 256), (256, 576))
WIDE = ((0, 256), (256, 640))
PACK = (128, 256)
WIN = 640


def halves(v):
    hi = v.astype(bf16)
    return hi, (v - hi.astype(f32)).astype(bf16)


def dot(a, b):
    return jnp.dot(a, b, preferred_element_type=f32)


def kernel(
    et_hbm, ev_ref, q_hbm, at_hbm, out_ref,
    et_v, q_v, at_v, eh, el, rot, act,
    ry_tx, ry_rx, rz_tx, rz_rx, st,
    pk_tx, pk_rx, px_tx, px_rx, pz_tx, pz_rx, pm, pc_rx, pc,
    sk_tx, sk_rx, sx_tx, sx_own, sx_rx, sz_tx, sz_own, sz_rx,
    load_sem, quad_tx, quad_rx, pair_tx, pair_rx, half_tx, half_rx, turn_tx, turn_rx, all_tx, all_rx, vouched,
):
    row, col = lax.axis_index("row"), lax.axis_index("col")
    y, zl = row // 4, row % 4
    zh, x, k = col // 8, (col // 2) % 4, col % 2

    def device(y=y, zl=zl, zh=zh, x=x, k=k):
        return (y * 4 + zl, zh * 8 + x * 2 + k)

    to_y = (y + x - zl + 6) % 4
    to_zl = (zh - y + 5 + zl // 2) % 4
    from_x = (x + y - zh + 6) % 4
    from_zh = (zh + zl + 7 - x // 2) % 4

    loads = [
        pltpu.make_async_copy(q_hbm, q_v, load_sem.at[0]),
        *(
            pltpu.make_async_copy(et_hbm.at[pl.ds(lo, hi - lo)], et_v.at[pl.ds(lo, hi - lo)], load_sem.at[1 + p])
            for p, (lo, hi) in enumerate(EIG)
        ),
        pltpu.make_async_copy(at_hbm, at_v.at[pl.ds(pl.multiple_of(k * 64, 64), COLS)], load_sem.at[3]),
    ]
    for load in loads[:3]:
        load.start()

    barrier = pltpu.get_barrier_semaphore()

    def greet(who):
        pl.semaphore_signal(barrier, inc=1, device_id=who, device_id_type=MESH)

    row_peers = [((y + dy) % 4, (zl + dz) % 4) for dz in (2, 1, 3, 0) for dy in (2, 1, 3, 0)][:15]
    for d in (1, 3):
        greet(device(zh=(zh + d) % 4))
    for d in (2, 1, 3):
        greet(device(zl=(zl + d) % 4))
        greet(device(y=(y + d) % 4))
        greet(device(x=(x + d) % 4))
    greet(device(k=1 - k))

    loads[3].start()
    at_v[pl.ds(pl.multiple_of((1 - k) * COLS, 64), 64), :] = jnp.zeros((64, 1024), bf16)

    loads[0].wait()
    qh, ql = halves(q_v[...])

    def rotated(p):
        lo, hi = EIG[p]
        loads[1 + p].wait()
        h, l = halves(et_v[lo:hi, :])
        eh[lo:hi, :] = h
        el[lo:hi, :] = l
        rot[lo:hi, :] = dot(h, qh) + dot(h, ql) + dot(l, qh)

    rotated(0)
    pl.semaphore_wait(barrier, 12)
    pl.semaphore_signal(vouched, inc=1, device_id=device(zh=(zh + 3) % 4), device_id_type=MESH)

    sent = []

    def send(src, dst, tx, rx, who):
        copy = pltpu.make_async_remote_copy(
            src_ref=src, dst_ref=dst, send_sem=tx, recv_sem=rx, device_id=who, device_id_type=MESH
        )
        copy.start()
        sent.append(copy)
        return copy

    def quad(stage, ch, part, source, target, axis, at):
        copies = []
        for d in range(1, 4):
            to = (at + d) % 4
            copies.append(
                send(source(to), target(d - 1), quad_tx.at[stage, ch, part, d - 1], quad_rx.at[stage, ch, part, d - 1],
                     device(**{axis: to}))
            )
        return copies

    def arrive(copies):
        for copy in copies:
            copy.wait_recv()

    def rotate(ch, p):
        lanes = slice(ch * QC, (ch + 1) * QC)
        lo, hi = EIG[p]
        near, far = (("zl", zl), ("y", y))[:: 1 if p == 0 else -1]
        tx, rx, tz, rz, s = ry_tx[p], ry_rx[p], rz_tx[p], rz_rx[p], st[p]
        i, j = near[1], far[1]
        tx[ch] = rot[lo:hi, lanes].T.reshape(4, 32, hi - lo)
        copies = quad(0, ch, p, lambda to: tx.at[ch, to], lambda n: rx.at[ch, n], *near)
        yield
        arrive(copies)
        total = tx[ch, i] + rx[ch, 0] + rx[ch, 1] + rx[ch, 2]
        tz[ch] = total.reshape(4, 8, hi - lo)
        copies = quad(1, ch, p, lambda to: tz.at[ch, to], lambda n: rz.at[ch, n], *far)
        yield
        arrive(copies)
        total = tz[ch, j] + rz[ch, 0] + rz[ch, 1] + rz[ch, 2]
        s[ch, i, j] = total / (ev_ref[...].reshape(1, COLS)[:, lo:hi] + damping)
        copies = quad(2, ch, p, lambda to: s.at[ch, i, j], lambda n: s.at[ch, i, j], *far)
        yield
        arrive(copies)
        copies = quad(3, ch, p, lambda to: s.at[ch, i], lambda n: s.at[ch, i], *near)
        yield
        arrive(copies)

    def expand(ch, part, state):
        lo, hi = EIG[part]
        sh, sl = halves(st[part][ch].reshape(QC, hi - lo))
        both = jnp.concatenate([sh, sl], axis=0)

        def window(at, p):
            first, last = WIDE[p]
            cols = pl.ds(pl.multiple_of(at * 512 + first, 128), last - first)
            wide = dot(both, eh[lo:hi, cols])
            return wide[:QC] + wide[QC:] + dot(sh, el[lo:hi, cols])

        for p in range(2):
            if part == 0:
                pk_tx[p][ch] = window(1 - k, p)
            else:
                pk_tx[p][ch] = pk_tx[p][ch] + window(1 - k, p)
                state[ch, p] = send(
                    pk_tx[p].at[ch], pk_rx[p].at[ch], pair_tx.at[p, ch], pair_rx.at[p, ch], device(k=1 - k)
                )
        for p in range(2):
            first, last = WIDE[p]
            own = window(k, p).reshape(4, 32, last - first)
            px_tx[p][ch] = own if part == 0 else px_tx[p][ch] + own

    def collect(ch, p, state):
        first, last = WIDE[p]
        width = last - first
        tx, rx, tz, rz = px_tx[p], px_rx[p], pz_tx[p], pz_rx[p]
        state[ch, p].wait_recv()
        tx[ch] = tx[ch] + pk_rx[p][ch].reshape(4, 32, width)
        copies = quad(4, ch, p, lambda to: tx.at[ch, to], lambda i: rx.at[ch, i], "x", x)
        yield
        arrive(copies)
        total = tx[ch, x] + rx[ch, 0] + rx[ch, 1] + rx[ch, 2]
        tz[ch] = total.reshape(4, 8, width)
        copies = quad(5, ch, p, lambda to: tz.at[ch, to], lambda i: rz.at[ch, i], "zh", zh)
        yield
        arrive(copies)
        total = tz[ch, zh] + rz[ch, 0] + rz[ch, 1] + rz[ch, 2]
        pm[p][ch] = jnp.concatenate([total[:, : PACK[p]], total[:, width - PACK[p] :]], axis=0).astype(bf16)
        moved = send(pm[p].at[ch], pc_rx[p].at[ch, x, zh], turn_tx.at[p, ch], turn_rx.at[p, ch],
                     device(x=zl, y=to_y, zh=y, zl=to_zl))
        yield
        moved.wait_recv()
        here = pc_rx[p].at[ch, from_x, from_zh]
        copies = []
        for n, (py, pz) in enumerate(row_peers):
            copies.append(send(here, here, all_tx.at[ch, p, n], all_rx.at[ch, p, n], device(y=py, zl=pz)))
        yield
        arrive(copies)
        for a in range(4):
            for b in range(4):
                v = pc_rx[p][ch, a, b].astype(f32)
                rows = slice(32 * a + 8 * b, 32 * a + 8 * b + 8)
                pc[ch, rows, first : first + PACK[p]] = v[0:8]
                pc[ch, rows, last - PACK[p] : last] = v[8:16]

    def score(ch, p, state):
        first, last = WIDE[p]
        precond = pc[ch, :, first:last].astype(bf16)

        def scores(core, half):
            tokens = act[core, half, :, :, :, first:last].reshape(256, last - first)
            return lax.dot_general(tokens, precond, (((1,), (1,)), ((), ())), preferred_element_type=f32)

        for h in range(2):
            if p == 0:
                sk_tx[ch, h] = scores(1 - k, h)
            else:
                sk_tx[ch, h] = sk_tx[ch, h] + scores(1 - k, h)
                state[ch, h] = send(
                    sk_tx.at[ch, h], sk_rx.at[ch, h], half_tx.at[ch, h], half_rx.at[ch, h], device(k=1 - k)
                )
        for h in range(2):
            own = scores(k, h).reshape(4, 64, QC)
            sx_own[ch, h] = own if p == 0 else sx_own[ch, h] + own

    def finish(ch, h, state):
        lanes = slice(ch * QC, (ch + 1) * QC)
        state[ch, h].wait_recv()
        total = sx_own[ch, h] + sk_rx[ch, h].reshape(4, 64, QC)
        sx_own[ch, h] = total
        sx_tx[ch, h] = total.astype(bf16)
        copies = quad(6, ch, h, lambda to: sx_tx.at[ch, h, to], lambda s: sx_rx.at[ch, h, s], "x", x)
        yield
        arrive(copies)
        total = sx_own[ch, h, x]
        for s in range(3):
            total = total + sx_rx[ch, h, s].astype(f32)
        total = total.reshape(4, 16, QC)
        sz_own[ch, h] = total
        sz_tx[ch, h] = total.astype(bf16)
        copies = quad(7, ch, h, lambda to: sz_tx.at[ch, h, to], lambda s: sz_rx.at[ch, h, s], "zh", zh)
        yield
        arrive(copies)
        total = sz_own[ch, h, zh]
        for s in range(3):
            total = total + sz_rx[ch, h, s].astype(f32)
        out_ref[16 * h : 16 * h + 16, lanes] = total

    def step(streams):
        for one in streams:
            next(one, None)

    summed = {}
    first = [[rotate(ch, p) for p in range(2)] for ch in range(CHUNKS)]
    step([first[0][0]])
    rotated(1)
    step([first[0][1], first[1][0], first[1][1]])
    for stage in range(1, 4):
        step(first[0] + first[1])
        if stage == 1:
            loads[3].wait()
            for t in range(8):
                block = at_v[:, t * 128 : (t + 1) * 128].T
                for i in range(4):
                    c = 4 * t + i
                    for h in range(2):
                        at = 32 * i + 16 * h
                        act[c % 2, h, (c // 2) % 4, c // 8] = block[at : at + 16]
    second = [[collect(ch, p, summed) for p in range(2)] for ch in range(CHUNKS)]
    for ch in range(CHUNKS):
        for p in range(2):
            step([first[ch][p]])
            expand(ch, p, summed)
        step(second[ch])
    pl.semaphore_wait(vouched, 1)
    for stage in range(1, 4):
        step(second[0] + second[1])
    third = [finish(ch, h, summed) for ch in range(CHUNKS) for h in range(2)]
    for ch in range(CHUNKS):
        for p in range(2):
            step([second[ch][p]])
            score(ch, p, summed)
        step(third[2 * ch : 2 * ch + 2])
    for copy in sent:
        copy.wait_send()
    sent.clear()
    step(third)
    step(third)
    for copy in sent:
        copy.wait_send()


def per_device(eigenbasis, eigenvalues, queries, activations):
    n = CHUNKS
    dma = pltpu.SemaphoreType.DMA
    V = pltpu.VMEM

    def parts(lanes, *lead):
        return [V((n, *lead, hi - lo), f32) for lo, hi in lanes]

    any_space = pl.BlockSpec(memory_space=pl.ANY)
    vmem = pl.BlockSpec(memory_space=V)
    return pl.pallas_call(
        kernel,
        out_shape=jax.ShapeDtypeStruct((32, 256), f32),
        in_specs=[any_space, vmem, any_space, any_space],
        out_specs=vmem,
        scratch_shapes=[
            V((COLS, 1152), f32), V((1152, 256), f32), V((WIN, 1024), bf16),
            V((COLS, 1152), bf16), V((COLS, 1152), bf16), V((COLS, 256), f32), V((2, 2, 4, 4, 16, WIN), bf16),
            parts(EIG, 4, 32), parts(EIG, 3, 32), parts(EIG, 4, 8), parts(EIG, 3, 8), parts(EIG, 4, 4, 8),
            parts(WIDE, QC), parts(WIDE, QC), parts(WIDE, 4, 32), parts(WIDE, 3, 32), parts(WIDE, 4, 8),
            parts(WIDE, 3, 8), [V((n, 16, w), bf16) for w in PACK], [V((n, 4, 4, 16, w), bf16) for w in PACK],
            V((n, QC, WIN), f32),
            V((n, 2, 256, QC), f32), V((n, 2, 256, QC), f32),
            V((n, 2, 4, 64, QC), bf16), V((n, 2, 4, 64, QC), f32), V((n, 2, 3, 64, QC), bf16),
            V((n, 2, 4, 16, QC), bf16), V((n, 2, 4, 16, QC), f32), V((n, 2, 3, 16, QC), bf16),
            dma((4,)), dma((8, n, 2, 3)), dma((8, n, 2, 3)), dma((2, n)), dma((2, n)), dma((n, 2)), dma((n, 2)),
            dma((2, n)), dma((2, n)), dma((n, 2, 15)), dma((n, 2, 15)),
            pltpu.SemaphoreType.REGULAR,
        ],
        compiler_params=pltpu.CompilerParams(
            collective_id=1, has_side_effects=True, vmem_limit_bytes=56 * 1024 * 1024
        ),
    )(eigenbasis.T, eigenvalues, queries, activations.T)


def solution(mesh):
    placed = (P("row", "col"), P("col"), P("row", None), P("row", "col"))
    return jax.shard_map(
        per_device, mesh=mesh, in_specs=placed, out_specs=P(("row", "col"), None), check_vma=False
    )
```

```python
import functools

import jax
import jax.numpy as jnp
from jax import lax
from jax.experimental import pallas as pl
from jax.experimental.pallas import tpu as pltpu
from jax.sharding import PartitionSpec as P

damping = 0.1
MESH = pl.DeviceIdType.MESH
f32, bf16 = jnp.float32, jnp.bfloat16
CHUNKS = 2
QC = 128
COLS = 576
EIG = ((0, 256), (256, 576))
WIDE = ((0, 256), (256, 640))
PACK = (128, 256)
WIN = 640


def halves(v):
    hi = v.astype(bf16)
    return hi, (v - hi.astype(f32)).astype(bf16)


def dot(a, b):
    return jnp.dot(a, b, preferred_element_type=f32)


def kernel(
    et_hbm, ev_ref, q_hbm, at_hbm, out_ref,
    et_v, q_v, at_v, eh, el, rot, act,
    ry_tx, ry_rx, rz_tx, rz_rx, st,
    pk_tx, pk_rx, px_tx, px_rx, pz_tx, pz_rx, pm, pc_rx, pc,
    sk_tx, sk_rx, sx_tx, sx_own, sx_rx, sz_tx, sz_own, sz_rx,
    load_sem, quad_tx, quad_rx, pair_tx, pair_rx, half_tx, half_rx, turn_tx, turn_rx, all_tx, all_rx, vouched,
):
    row, col = lax.axis_index("row"), lax.axis_index("col")
    y, zl = row // 4, row % 4
    zh, x, k = col // 8, (col // 2) % 4, col % 2

    def device(y=y, zl=zl, zh=zh, x=x, k=k):
        return (y * 4 + zl, zh * 8 + x * 2 + k)

    to_y = (y + x - zl + 6) % 4
    to_zl = (zh - y + 5 + zl // 2) % 4
    from_x = (x + y - zh + 6) % 4
    from_zh = (zh + zl + 7 - x // 2) % 4

    loads = [
        pltpu.make_async_copy(q_hbm, q_v, load_sem.at[0]),
        *(
            pltpu.make_async_copy(et_hbm.at[pl.ds(lo, hi - lo)], et_v.at[pl.ds(lo, hi - lo)], load_sem.at[1 + p])
            for p, (lo, hi) in enumerate(EIG)
        ),
        pltpu.make_async_copy(at_hbm, at_v.at[pl.ds(pl.multiple_of(k * 64, 64), COLS)], load_sem.at[3]),
    ]
    for load in loads[:3]:
        load.start()

    barrier = pltpu.get_barrier_semaphore()

    def greet(who):
        pl.semaphore_signal(barrier, inc=1, device_id=who, device_id_type=MESH)

    row_peers = [((y + dy) % 4, (zl + dz) % 4) for dz in (2, 1, 3, 0) for dy in (2, 1, 3, 0)][:15]
    for d in (1, 3):
        greet(device(zh=(zh + d) % 4))
    for d in (2, 1, 3):
        greet(device(zl=(zl + d) % 4))
        greet(device(y=(y + d) % 4))
        greet(device(x=(x + d) % 4))
    greet(device(k=1 - k))

    loads[3].start()
    at_v[pl.ds(pl.multiple_of((1 - k) * COLS, 64), 64), :] = jnp.zeros((64, 1024), bf16)

    loads[0].wait()
    qh, ql = halves(q_v[...])

    def rotated(p):
        lo, hi = EIG[p]
        loads[1 + p].wait()
        h, l = halves(et_v[lo:hi, :])
        eh[lo:hi, :] = h
        el[lo:hi, :] = l
        rot[lo:hi, :] = dot(h, qh) + dot(h, ql) + dot(l, qh)

    rotated(0)
    pl.semaphore_wait(barrier, 12)
    pl.semaphore_signal(vouched, inc=1, device_id=device(zh=(zh + 3) % 4), device_id_type=MESH)

    sent = []

    def send(src, dst, tx, rx, who):
        copy = pltpu.make_async_remote_copy(
            src_ref=src, dst_ref=dst, send_sem=tx, recv_sem=rx, device_id=who, device_id_type=MESH
        )
        copy.start()
        sent.append(copy)
        return copy

    def quad(stage, ch, part, source, target, axis, at):
        copies = []
        for d in (2, 1, 3):
            to = (at + d) % 4
            copies.append(
                send(source(to), target(d - 1), quad_tx.at[stage, ch, part, d - 1], quad_rx.at[stage, ch, part, d - 1],
                     device(**{axis: to}))
            )
        return copies

    def arrive(copies):
        for copy in copies:
            copy.wait_recv()

    def rotate(ch, p):
        lanes = slice(ch * QC, (ch + 1) * QC)
        lo, hi = EIG[p]
        near, far = (("zl", zl), ("y", y))[:: 1 if p == 0 else -1]
        tx, rx, tz, rz, s = ry_tx[p], ry_rx[p], rz_tx[p], rz_rx[p], st[p]
        i, j = near[1], far[1]
        tx[ch] = rot[lo:hi, lanes].T.reshape(4, 32, hi - lo)
        copies = quad(0, ch, p, lambda to: tx.at[ch, to], lambda n: rx.at[ch, n], *near)
        yield
        arrive(copies)
        total = tx[ch, i] + rx[ch, 0] + rx[ch, 1] + rx[ch, 2]
        tz[ch] = total.reshape(4, 8, hi - lo)
        copies = quad(1, ch, p, lambda to: tz.at[ch, to], lambda n: rz.at[ch, n], *far)
        yield
        arrive(copies)
        total = tz[ch, j] + rz[ch, 0] + rz[ch, 1] + rz[ch, 2]
        s[ch, i, j] = total / (ev_ref[...].reshape(1, COLS)[:, lo:hi] + damping)
        copies = quad(2, ch, p, lambda to: s.at[ch, i, j], lambda n: s.at[ch, i, j], *far)
        yield
        arrive(copies)
        copies = quad(3, ch, p, lambda to: s.at[ch, i], lambda n: s.at[ch, i], *near)
        yield
        arrive(copies)

    def expand(ch, part, state):
        lo, hi = EIG[part]
        sh, sl = halves(st[part][ch].reshape(QC, hi - lo))
        both = jnp.concatenate([sh, sl], axis=0)

        def window(at, p):
            first, last = WIDE[p]
            cols = pl.ds(pl.multiple_of(at * 512 + first, 128), last - first)
            wide = dot(both, eh[lo:hi, cols])
            return wide[:QC] + wide[QC:] + dot(sh, el[lo:hi, cols])

        for p in range(2):
            if part == 0:
                pk_tx[p][ch] = window(1 - k, p)
            else:
                pk_tx[p][ch] = pk_tx[p][ch] + window(1 - k, p)
                state[ch, p] = send(
                    pk_tx[p].at[ch], pk_rx[p].at[ch], pair_tx.at[p, ch], pair_rx.at[p, ch], device(k=1 - k)
                )
        for p in range(2):
            first, last = WIDE[p]
            own = window(k, p).reshape(4, 32, last - first)
            px_tx[p][ch] = own if part == 0 else px_tx[p][ch] + own

    def collect(ch, p, state):
        first, last = WIDE[p]
        width = last - first
        tx, rx, tz, rz = px_tx[p], px_rx[p], pz_tx[p], pz_rx[p]
        state[ch, p].wait_recv()
        tx[ch] = tx[ch] + pk_rx[p][ch].reshape(4, 32, width)
        copies = quad(4, ch, p, lambda to: tx.at[ch, to], lambda i: rx.at[ch, i], "x", x)
        yield
        arrive(copies)
        total = tx[ch, x] + rx[ch, 0] + rx[ch, 1] + rx[ch, 2]
        tz[ch] = total.reshape(4, 8, width)
        copies = quad(5, ch, p, lambda to: tz.at[ch, to], lambda i: rz.at[ch, i], "zh", zh)
        yield
        arrive(copies)
        total = tz[ch, zh] + rz[ch, 0] + rz[ch, 1] + rz[ch, 2]
        pm[p][ch] = jnp.concatenate([total[:, : PACK[p]], total[:, width - PACK[p] :]], axis=0).astype(bf16)
        moved = send(pm[p].at[ch], pc_rx[p].at[ch, x, zh], turn_tx.at[p, ch], turn_rx.at[p, ch],
                     device(x=zl, y=to_y, zh=y, zl=to_zl))
        yield
        moved.wait_recv()
        here = pc_rx[p].at[ch, from_x, from_zh]
        copies = []
        for n, (py, pz) in enumerate(row_peers):
            copies.append(send(here, here, all_tx.at[ch, p, n], all_rx.at[ch, p, n], device(y=py, zl=pz)))
        yield
        arrive(copies)
        for a in range(4):
            for b in range(4):
                v = pc_rx[p][ch, a, b].astype(f32)
                rows = slice(32 * a + 8 * b, 32 * a + 8 * b + 8)
                pc[ch, rows, first : first + PACK[p]] = v[0:8]
                pc[ch, rows, last - PACK[p] : last] = v[8:16]

    def score(ch, p, state):
        first, last = WIDE[p]
        precond = pc[ch, :, first:last].astype(bf16)

        def scores(core, half):
            tokens = act[core, half, :, :, :, first:last].reshape(256, last - first)
            return lax.dot_general(tokens, precond, (((1,), (1,)), ((), ())), preferred_element_type=f32)

        for h in range(2):
            if p == 0:
                sk_tx[ch, h] = scores(1 - k, h)
            else:
                sk_tx[ch, h] = sk_tx[ch, h] + scores(1 - k, h)
                state[ch, h] = send(
                    sk_tx.at[ch, h], sk_rx.at[ch, h], half_tx.at[ch, h], half_rx.at[ch, h], device(k=1 - k)
                )
        for h in range(2):
            own = scores(k, h).reshape(4, 64, QC)
            sx_own[ch, h] = own if p == 0 else sx_own[ch, h] + own

    def finish(ch, h, state):
        lanes = slice(ch * QC, (ch + 1) * QC)
        state[ch, h].wait_recv()
        total = sx_own[ch, h] + sk_rx[ch, h].reshape(4, 64, QC)
        sx_own[ch, h] = total
        sx_tx[ch, h] = total.astype(bf16)
        copies = quad(6, ch, h, lambda to: sx_tx.at[ch, h, to], lambda s: sx_rx.at[ch, h, s], "x", x)
        yield
        arrive(copies)
        total = sx_own[ch, h, x]
        for s in range(3):
            total = total + sx_rx[ch, h, s].astype(f32)
        total = total.reshape(4, 16, QC)
        sz_own[ch, h] = total
        sz_tx[ch, h] = total.astype(bf16)
        copies = quad(7, ch, h, lambda to: sz_tx.at[ch, h, to], lambda s: sz_rx.at[ch, h, s], "zh", zh)
        yield
        arrive(copies)
        total = sz_own[ch, h, zh]
        for s in range(3):
            total = total + sz_rx[ch, h, s].astype(f32)
        out_ref[16 * h : 16 * h + 16, lanes] = total

    def lay_tokens():
        loads[3].wait()
        for t in range(8):
            block = at_v[:, t * 128 : (t + 1) * 128].T
            for i in range(4):
                c = 4 * t + i
                for h in range(2):
                    at = 32 * i + 16 * h
                    act[c % 2, h, (c // 2) % 4, c // 8] = block[at : at + 16]

    def left():
        for copy in sent:
            copy.wait_send()
        sent.clear()

    def step(streams):
        for one in streams:
            next(one, None)

    summed = {}
    first = [[rotate(ch, p) for p in range(2)] for ch in range(CHUNKS)]
    step([first[0][0]])
    rotated(1)
    step([first[0][1], first[1][0], first[1][1]])
    for stage in range(1, 4):
        step(first[0] + first[1])
    second = [[collect(ch, p, summed) for p in range(2)] for ch in range(CHUNKS)]
    for ch in range(CHUNKS):
        for p in range(2):
            step([first[ch][p]])
            expand(ch, p, summed)
        step(second[ch])
    pl.semaphore_wait(vouched, 1)
    for stage in range(1, 4):
        step(second[0] + second[1])
        if stage == 1:
            lay_tokens()
            left()
    third = [finish(ch, h, summed) for ch in range(CHUNKS) for h in range(2)]
    for ch in range(CHUNKS):
        for p in range(2):
            step([second[ch][p]])
            score(ch, p, summed)
        step(third[2 * ch : 2 * ch + 2])
    step(third)
    left()
    step(third)


def per_device(eigenbasis, eigenvalues, queries, activations):
    n = CHUNKS
    dma = pltpu.SemaphoreType.DMA
    V = pltpu.VMEM

    def parts(lanes, *lead):
        return [V((n, *lead, hi - lo), f32) for lo, hi in lanes]

    any_space = pl.BlockSpec(memory_space=pl.ANY)
    vmem = pl.BlockSpec(memory_space=V)
    return pl.pallas_call(
        kernel,
        out_shape=jax.ShapeDtypeStruct((32, 256), f32),
        in_specs=[any_space, vmem, any_space, any_space],
        out_specs=vmem,
        scratch_shapes=[
            V((COLS, 1152), f32), V((1152, 256), f32), V((WIN, 1024), bf16),
            V((COLS, 1152), bf16), V((COLS, 1152), bf16), V((COLS, 256), f32), V((2, 2, 4, 4, 16, WIN), bf16),
            parts(EIG, 4, 32), parts(EIG, 3, 32), parts(EIG, 4, 8), parts(EIG, 3, 8), parts(EIG, 4, 4, 8),
            parts(WIDE, QC), parts(WIDE, QC), parts(WIDE, 4, 32), parts(WIDE, 3, 32), parts(WIDE, 4, 8),
            parts(WIDE, 3, 8), [V((n, 16, w), bf16) for w in PACK], [V((n, 4, 4, 16, w), bf16) for w in PACK],
            V((n, QC, WIN), f32),
            V((n, 2, 256, QC), f32), V((n, 2, 256, QC), f32),
            V((n, 2, 4, 64, QC), bf16), V((n, 2, 4, 64, QC), f32), V((n, 2, 3, 64, QC), bf16),
            V((n, 2, 4, 16, QC), bf16), V((n, 2, 4, 16, QC), f32), V((n, 2, 3, 16, QC), bf16),
            dma((4,)), dma((8, n, 2, 3)), dma((8, n, 2, 3)), dma((2, n)), dma((2, n)), dma((n, 2)), dma((n, 2)),
            dma((2, n)), dma((2, n)), dma((n, 2, 15)), dma((n, 2, 15)),
            pltpu.SemaphoreType.REGULAR,
        ],
        compiler_params=pltpu.CompilerParams(
            collective_id=1, has_side_effects=True, vmem_limit_bytes=56 * 1024 * 1024
        ),
    )(eigenbasis.T, eigenvalues, queries, activations.T)


def solution(mesh):
    placed = (P("row", "col"), P("col"), P("row", None), P("row", "col"))
    return jax.shard_map(
        per_device, mesh=mesh, in_specs=placed, out_specs=P(("row", "col"), None), check_vma=False
    )
```

```python
import functools

import jax
import jax.numpy as jnp
from jax import lax
from jax.experimental import pallas as pl
from jax.experimental.pallas import tpu as pltpu
from jax.sharding import PartitionSpec as P

damping = 0.1
MESH = pl.DeviceIdType.MESH
f32, bf16 = jnp.float32, jnp.bfloat16
CHUNKS = 2
QC = 128
COLS = 576
EIG = ((0, 256), (256, 576))
WIDE = ((0, 384), (384, 640))
PACK = (256, 128)
WIN = 640


def halves(v):
    hi = v.astype(bf16)
    return hi, (v - hi.astype(f32)).astype(bf16)


def dot(a, b):
    return jnp.dot(a, b, preferred_element_type=f32)


def kernel(
    et_hbm, ev_ref, q_hbm, at_hbm, out_ref,
    et_v, q_v, at_v, eh, el, rot, act,
    ry_tx, ry_rx, rz_tx, rz_rx, st,
    pk_tx, pk_rx, px_tx, px_rx, pz_tx, pz_rx, pm, pc_rx, pc,
    sk_tx, sk_rx, sx_tx, sx_own, sx_rx, sz_tx, sz_own, sz_rx,
    load_sem, quad_tx, quad_rx, pair_tx, pair_rx, half_tx, half_rx, turn_tx, turn_rx, all_tx, all_rx, vouched,
):
    row, col = lax.axis_index("row"), lax.axis_index("col")
    y, zl = row // 4, row % 4
    zh, x, k = col // 8, (col // 2) % 4, col % 2

    def device(y=y, zl=zl, zh=zh, x=x, k=k):
        return (y * 4 + zl, zh * 8 + x * 2 + k)

    to_y = (y + x - zl + 6) % 4
    to_zl = (zh - y + 5 + zl // 2) % 4
    from_x = (x + y - zh + 6) % 4
    from_zh = (zh + zl + 7 - x // 2) % 4

    loads = [
        pltpu.make_async_copy(q_hbm, q_v, load_sem.at[0]),
        *(
            pltpu.make_async_copy(et_hbm.at[pl.ds(lo, hi - lo)], et_v.at[pl.ds(lo, hi - lo)], load_sem.at[1 + p])
            for p, (lo, hi) in enumerate(EIG)
        ),
        pltpu.make_async_copy(at_hbm, at_v.at[pl.ds(pl.multiple_of(k * 64, 64), COLS)], load_sem.at[3]),
    ]
    for load in loads[:3]:
        load.start()

    barrier = pltpu.get_barrier_semaphore()

    def greet(who):
        pl.semaphore_signal(barrier, inc=1, device_id=who, device_id_type=MESH)

    row_peers = [((y + dy) % 4, (zl + dz) % 4) for dz in (2, 1, 3, 0) for dy in (2, 1, 3, 0)][:15]
    for d in (1, 3):
        greet(device(zh=(zh + d) % 4))
    for d in (2, 1, 3):
        greet(device(zl=(zl + d) % 4))
        greet(device(y=(y + d) % 4))
        greet(device(x=(x + d) % 4))
    greet(device(k=1 - k))

    loads[3].start()
    at_v[pl.ds(pl.multiple_of((1 - k) * COLS, 64), 64), :] = jnp.zeros((64, 1024), bf16)

    loads[0].wait()
    qh, ql = halves(q_v[...])

    def rotated(p):
        lo, hi = EIG[p]
        loads[1 + p].wait()
        h, l = halves(et_v[lo:hi, :])
        eh[lo:hi, :] = h
        el[lo:hi, :] = l
        rot[lo:hi, :] = dot(h, qh) + dot(h, ql) + dot(l, qh)

    rotated(0)
    pl.semaphore_wait(barrier, 12)
    pl.semaphore_signal(vouched, inc=1, device_id=device(zh=(zh + 3) % 4), device_id_type=MESH)

    sent = []

    def send(src, dst, tx, rx, who):
        copy = pltpu.make_async_remote_copy(
            src_ref=src, dst_ref=dst, send_sem=tx, recv_sem=rx, device_id=who, device_id_type=MESH
        )
        copy.start()
        sent.append(copy)
        return copy

    def quad(stage, ch, part, source, target, axis, at):
        copies = []
        for d in (2, 1, 3):
            to = (at + d) % 4
            copies.append(
                send(source(to), target(d - 1), quad_tx.at[stage, ch, part, d - 1], quad_rx.at[stage, ch, part, d - 1],
                     device(**{axis: to}))
            )
        return copies

    def arrive(copies):
        for copy in copies:
            copy.wait_recv()

    def rotate(ch, p):
        lanes = slice(ch * QC, (ch + 1) * QC)
        lo, hi = EIG[p]
        near, far = (("zl", zl), ("y", y))[:: 1 if p == 0 else -1]
        tx, rx, tz, rz, s = ry_tx[p], ry_rx[p], rz_tx[p], rz_rx[p], st[p]
        i, j = near[1], far[1]
        tx[ch] = rot[lo:hi, lanes].T.reshape(4, 32, hi - lo)
        copies = quad(0, ch, p, lambda to: tx.at[ch, to], lambda n: rx.at[ch, n], *near)
        yield
        arrive(copies)
        total = tx[ch, i] + rx[ch, 0] + rx[ch, 1] + rx[ch, 2]
        tz[ch] = total.reshape(4, 8, hi - lo)
        copies = quad(1, ch, p, lambda to: tz.at[ch, to], lambda n: rz.at[ch, n], *far)
        yield
        arrive(copies)
        total = tz[ch, j] + rz[ch, 0] + rz[ch, 1] + rz[ch, 2]
        s[ch, i, j] = total / (ev_ref[...].reshape(1, COLS)[:, lo:hi] + damping)
        copies = quad(2, ch, p, lambda to: s.at[ch, i, j], lambda n: s.at[ch, i, j], *far)
        yield
        arrive(copies)
        copies = quad(3, ch, p, lambda to: s.at[ch, i], lambda n: s.at[ch, i], *near)
        yield
        arrive(copies)

    def expand(ch, part, state):
        lo, hi = EIG[part]
        sh, sl = halves(st[part][ch].reshape(QC, hi - lo))
        both = jnp.concatenate([sh, sl], axis=0)

        def window(at, p):
            first, last = WIDE[p]
            cols = pl.ds(pl.multiple_of(at * 512 + first, 128), last - first)
            wide = dot(both, eh[lo:hi, cols])
            return wide[:QC] + wide[QC:] + dot(sh, el[lo:hi, cols])

        for p in range(2):
            if part == 0:
                pk_tx[p][ch] = window(1 - k, p)
            else:
                pk_tx[p][ch] = pk_tx[p][ch] + window(1 - k, p)
                state[ch, p] = send(
                    pk_tx[p].at[ch], pk_rx[p].at[ch], pair_tx.at[p, ch], pair_rx.at[p, ch], device(k=1 - k)
                )
        for p in range(2):
            first, last = WIDE[p]
            own = window(k, p).reshape(4, 32, last - first)
            px_tx[p][ch] = own if part == 0 else px_tx[p][ch] + own

    def collect(ch, p, state):
        first, last = WIDE[p]
        width = last - first
        tx, rx, tz, rz = px_tx[p], px_rx[p], pz_tx[p], pz_rx[p]
        state[ch, p].wait_recv()
        tx[ch] = tx[ch] + pk_rx[p][ch].reshape(4, 32, width)
        copies = quad(4, ch, p, lambda to: tx.at[ch, to], lambda i: rx.at[ch, i], "x", x)
        yield
        arrive(copies)
        total = tx[ch, x] + rx[ch, 0] + rx[ch, 1] + rx[ch, 2]
        tz[ch] = total.reshape(4, 8, width)
        copies = quad(5, ch, p, lambda to: tz.at[ch, to], lambda i: rz.at[ch, i], "zh", zh)
        yield
        arrive(copies)
        total = tz[ch, zh] + rz[ch, 0] + rz[ch, 1] + rz[ch, 2]
        pm[p][ch] = jnp.concatenate([total[:, : PACK[p]], total[:, width - PACK[p] :]], axis=0).astype(bf16)
        moved = send(pm[p].at[ch], pc_rx[p].at[ch, x, zh], turn_tx.at[p, ch], turn_rx.at[p, ch],
                     device(x=zl, y=to_y, zh=y, zl=to_zl))
        yield
        moved.wait_recv()
        here = pc_rx[p].at[ch, from_x, from_zh]
        copies = []
        for n, (py, pz) in enumerate(row_peers):
            copies.append(send(here, here, all_tx.at[ch, p, n], all_rx.at[ch, p, n], device(y=py, zl=pz)))
        yield
        arrive(copies)
        for a in range(4):
            for b in range(4):
                v = pc_rx[p][ch, a, b].astype(f32)
                rows = slice(32 * a + 8 * b, 32 * a + 8 * b + 8)
                pc[ch, rows, first : first + PACK[p]] = v[0:8]
                pc[ch, rows, last - PACK[p] : last] = v[8:16]

    def score(ch, p, state):
        first, last = WIDE[p]
        precond = pc[ch, :, first:last].astype(bf16)

        def scores(core, half):
            tokens = act[core, half, :, :, :, first:last].reshape(256, last - first)
            return lax.dot_general(tokens, precond, (((1,), (1,)), ((), ())), preferred_element_type=f32)

        for h in range(2):
            if p == 0:
                sk_tx[ch, h] = scores(1 - k, h)
            else:
                sk_tx[ch, h] = sk_tx[ch, h] + scores(1 - k, h)
                state[ch, h] = send(
                    sk_tx.at[ch, h], sk_rx.at[ch, h], half_tx.at[ch, h], half_rx.at[ch, h], device(k=1 - k)
                )
        for h in range(2):
            own = scores(k, h).reshape(4, 64, QC)
            sx_own[ch, h] = own if p == 0 else sx_own[ch, h] + own

    def finish(ch, h, state):
        lanes = slice(ch * QC, (ch + 1) * QC)
        state[ch, h].wait_recv()
        total = sx_own[ch, h] + sk_rx[ch, h].reshape(4, 64, QC)
        sx_own[ch, h] = total
        sx_tx[ch, h] = total.astype(bf16)
        copies = quad(6, ch, h, lambda to: sx_tx.at[ch, h, to], lambda s: sx_rx.at[ch, h, s], "x", x)
        yield
        arrive(copies)
        total = sx_own[ch, h, x]
        for s in range(3):
            total = total + sx_rx[ch, h, s].astype(f32)
        total = total.reshape(4, 16, QC)
        sz_own[ch, h] = total
        sz_tx[ch, h] = total.astype(bf16)
        copies = quad(7, ch, h, lambda to: sz_tx.at[ch, h, to], lambda s: sz_rx.at[ch, h, s], "zh", zh)
        yield
        arrive(copies)
        total = sz_own[ch, h, zh]
        for s in range(3):
            total = total + sz_rx[ch, h, s].astype(f32)
        out_ref[16 * h : 16 * h + 16, lanes] = total

    def lay_tokens():
        loads[3].wait()
        for t in range(8):
            block = at_v[:, t * 128 : (t + 1) * 128].T
            for i in range(4):
                c = 4 * t + i
                for h in range(2):
                    at = 32 * i + 16 * h
                    act[c % 2, h, (c // 2) % 4, c // 8] = block[at : at + 16]

    def left():
        for copy in sent:
            copy.wait_send()
        sent.clear()

    def step(streams):
        for one in streams:
            next(one, None)

    summed = {}
    first = [[rotate(ch, p) for p in range(2)] for ch in range(CHUNKS)]
    step([first[0][0]])
    rotated(1)
    step([first[0][1], first[1][0], first[1][1]])
    for stage in range(1, 4):
        step(first[0] + first[1])
    second = [[collect(ch, p, summed) for p in range(2)] for ch in range(CHUNKS)]
    for ch in range(CHUNKS):
        for p in range(2):
            step([first[ch][p]])
            expand(ch, p, summed)
        step(second[ch])
    pl.semaphore_wait(vouched, 1)
    for stage in range(1, 4):
        step(second[0] + second[1])
        if stage == 1:
            lay_tokens()
            left()
    third = [finish(ch, h, summed) for ch in range(CHUNKS) for h in range(2)]
    for ch in range(CHUNKS):
        for p in range(2):
            step([second[ch][p]])
            score(ch, p, summed)
        step(third[2 * ch : 2 * ch + 2])
    step(third)
    left()
    step(third)


def per_device(eigenbasis, eigenvalues, queries, activations):
    n = CHUNKS
    dma = pltpu.SemaphoreType.DMA
    V = pltpu.VMEM

    def parts(lanes, *lead):
        return [V((n, *lead, hi - lo), f32) for lo, hi in lanes]

    any_space = pl.BlockSpec(memory_space=pl.ANY)
    vmem = pl.BlockSpec(memory_space=V)
    return pl.pallas_call(
        kernel,
        out_shape=jax.ShapeDtypeStruct((32, 256), f32),
        in_specs=[any_space, vmem, any_space, any_space],
        out_specs=vmem,
        scratch_shapes=[
            V((COLS, 1152), f32), V((1152, 256), f32), V((WIN, 1024), bf16),
            V((COLS, 1152), bf16), V((COLS, 1152), bf16), V((COLS, 256), f32), V((2, 2, 4, 4, 16, WIN), bf16),
            parts(EIG, 4, 32), parts(EIG, 3, 32), parts(EIG, 4, 8), parts(EIG, 3, 8), parts(EIG, 4, 4, 8),
            parts(WIDE, QC), parts(WIDE, QC), parts(WIDE, 4, 32), parts(WIDE, 3, 32), parts(WIDE, 4, 8),
            parts(WIDE, 3, 8), [V((n, 16, w), bf16) for w in PACK], [V((n, 4, 4, 16, w), bf16) for w in PACK],
            V((n, QC, WIN), f32),
            V((n, 2, 256, QC), f32), V((n, 2, 256, QC), f32),
            V((n, 2, 4, 64, QC), bf16), V((n, 2, 4, 64, QC), f32), V((n, 2, 3, 64, QC), bf16),
            V((n, 2, 4, 16, QC), bf16), V((n, 2, 4, 16, QC), f32), V((n, 2, 3, 16, QC), bf16),
            dma((4,)), dma((8, n, 2, 3)), dma((8, n, 2, 3)), dma((2, n)), dma((2, n)), dma((n, 2)), dma((n, 2)),
            dma((2, n)), dma((2, n)), dma((n, 2, 15)), dma((n, 2, 15)),
            pltpu.SemaphoreType.REGULAR,
        ],
        compiler_params=pltpu.CompilerParams(
            collective_id=1, has_side_effects=True, vmem_limit_bytes=56 * 1024 * 1024
        ),
    )(eigenbasis.T, eigenvalues, queries, activations.T)


def solution(mesh):
    placed = (P("row", "col"), P("col"), P("row", None), P("row", "col"))
    return jax.shard_map(
        per_device, mesh=mesh, in_specs=placed, out_specs=P(("row", "col"), None), check_vma=False
    )
```
